128 devices in a mesh: dp: 2 (over x_lo), label: 64 (over y, z, x_hi, core).
Axes of the slice: x: 4 (x_hi: 2, x_lo: 2; x = x_hi * 2 + x_lo), y: 4, z: 4, core: 2. Of those that a mesh axis runs over, the one named last changes fastest.
Arguments:
- hidden: bfloat16 [2048, 768], P(('dp', 'label')), may hold values from -6 to 6
- enc_weight: bfloat16 [768, 768], replicated, may hold values from -0.21875 to 0.21875
- cls_weight: bfloat16 [768, 196608], P(None, 'label'), may hold values from -0.21875 to 0.21875
- targets: int32 [2048, 196608], P('dp', 'label'), may hold values 0 or 1
Outputs:
- cls_grad: bfloat16 [768, 196608], P('dp', 'label')
- input_grad: bfloat16 [2048, 768], P(('dp', 'label'))
- enc_grad: float32 [768, 768], replicated
The draws below stay inside these ranges and needn't reach their ends.
All inputs are finite; a program needn't handle non-finite values. No bound on the sum of `targets` on one device may be relied on, other than what follows from the above.
Results may differ from the reference program's by a relative error of at most 0.012.
Values may be sent and summed in bfloat16 or wider, within the bound.
No kernel may reach another device: no remote copies, remote signals or barrier semaphores. Data moves between devices by JAX's collectives and lax.ppermute only.
A program may use at most 128 MiB of HBM per device.

```python
import jax
import jax.numpy as jnp
from jax import lax

D = 768
LAB_DEV = 3072
LABELS = 196608
BATCH = 2048
N_LABEL = 64


def place_ends(drawn, rng, low, largest):
    index_at = [jax.random.randint(jax.random.fold_in(rng, axis), (), 0, length) for axis, length in enumerate(drawn.shape)]
    main_axis = drawn.shape.index(max(drawn.shape))
    neighbour = index_at[:main_axis] + [(index_at[main_axis] + 1) % drawn.shape[main_axis]] + index_at[main_axis + 1:]
    return drawn.at[tuple(index_at)].set(low).at[tuple(neighbour)].set(largest)


def steps_of(key, shape, pieces, low, largest):
    gain = 1.0
    for position, blocks in pieces:
        steps = jax.random.uniform(jax.random.fold_in(jax.random.fold_in(key, 6), position), (blocks,), jnp.float32, low / len(pieces), largest / len(pieces))
        gain = gain * jnp.repeat(jnp.exp(steps), shape[position] // blocks).reshape((-1,) + (1,) * (len(shape) - 1 - position))
    return gain


def normal_values(stream_key, dims, spread, limit, cuts=(), kind=jnp.bfloat16):
    result = jax.random.normal(stream_key, dims, jnp.float32) * spread
    if len(cuts) > 0:
        result = steps_of(stream_key, dims, cuts, -0.22, 0.18) * result
    return jnp.clip(result, min=-limit, max=limit).astype(kind)


def setup_inputs(seed: int = 0) -> dict:
    key_list = jax.random.split(jax.random.key(seed), 5)
    hidden = normal_values(key_list[0], (BATCH, D), 1.0, 6.0, ((0, 128),))
    enc_weight = normal_values(key_list[1], (D, D), D ** -0.5, 0.21875)
    cls_weight = normal_values(key_list[2], (D, LABELS), D ** -0.5, 0.21875, ((1, 64),))
    targets = place_ends((jax.random.randint(key_list[3], (BATCH, LABELS), 0, 16) < 1).astype(jnp.int32), jax.random.fold_in(key_list[3], 1), 0, 1)
    return dict(hidden=hidden, enc_weight=enc_weight, cls_weight=cls_weight, targets=targets)


def reference(hidden, enc_weight, cls_weight, targets):
    pre = jnp.dot(hidden, enc_weight, preferred_element_type=jnp.float32)
    act = jnp.tanh(pre)
    emb = (hidden.astype(jnp.float32) + act).astype(jnp.bfloat16)
    scale = 1.0 / jnp.sqrt(jnp.float32(BATCH))
    weight_blocks = cls_weight.reshape(D, N_LABEL, LAB_DEV).transpose(1, 0, 2)
    target_blocks = targets.reshape(BATCH, N_LABEL, LAB_DEV).transpose(1, 0, 2)

    def one_block(total, block):
        weights, labels = block
        logits = jnp.dot(emb, weights, preferred_element_type=jnp.float32)
        err = ((jax.nn.sigmoid(logits) - labels.astype(jnp.float32)) * scale).astype(jnp.bfloat16)
        grad = jnp.dot(emb.T, err, preferred_element_type=jnp.float32).astype(jnp.bfloat16)
        total = total + jnp.dot(err, weights.T, preferred_element_type=jnp.float32)
        return (total, grad)
    emb_grad, grads = lax.scan(one_block, jnp.zeros((BATCH, D), jnp.float32), (weight_blocks, target_blocks))
    cls_grad = grads.transpose(1, 0, 2).reshape(D, LABELS)
    pre_grad = (emb_grad * (1.0 - act * act)).astype(jnp.bfloat16)
    input_grad = (emb_grad + jnp.dot(pre_grad, enc_weight.T, preferred_element_type=jnp.float32)).astype(jnp.bfloat16)
    enc_grad = jnp.dot(hidden.T, pre_grad, preferred_element_type=jnp.float32)
    return (cls_grad, input_grad, enc_grad)
```

```python
import jax
import jax.numpy as jnp
from jax import lax
from jax.sharding import Mesh, PartitionSpec as P

F32 = jnp.float32
BF16 = jnp.bfloat16
AXES = ("xl", "y", "z", "xh", "c")
N_CHUNK = 4


def dot(a, b, dims):
    return lax.dot_general(a, b, (dims, ((), ())), preferred_element_type=F32)


def swap(x, axis):
    return lax.ppermute(x, axis, [(0, 1), (1, 0)])


def body(hidden, enc_weight, cls_weight, targets):
    core = lax.axis_index("c")
    dp = lax.axis_index("xl")
    rows, width = hidden.shape
    labels = cls_weight.shape[1]
    half = width // 2
    n_peer = 32
    scale = 1.0 / jnp.sqrt(F32(2048))

    mine = lax.all_to_all(
        jnp.broadcast_to(hidden[None], (n_peer, rows, width)), ("y", "z", "xh"), 0, 0, tiled=True
    )
    other = swap(mine, "c")
    pair = jnp.where(core == 0, jnp.stack([mine, other], 1), jnp.stack([other, mine], 1))
    hid = pair.reshape(-1, width)
    act = jnp.tanh(dot(hid, enc_weight, ((1,), (0,))))
    emb = (hid.astype(F32) + act).astype(BF16)
    slope = 1.0 - act * act
    emb_send = lax.dynamic_slice(emb, (0, (1 - dp) * half), (emb.shape[0], half))
    emb_keep = lax.dynamic_slice(emb, (0, dp * half), (emb.shape[0], half))

    step = labels // N_CHUNK
    part = jnp.zeros((emb.shape[0], width), F32)
    errs, arrived = [], []
    for j in range(N_CHUNK):
        w = cls_weight[:, j * step : (j + 1) * step]
        t = targets[:, j * step : (j + 1) * step]
        logits = dot(emb, w, ((1,), (0,)))
        err = ((jax.nn.sigmoid(logits) - t.astype(F32)) * scale).astype(BF16)
        errs.append(err)
        arrived.append(swap(dot(emb_send, err, ((0,), (0,))).astype(BF16), "xl"))
        part = part + dot(err, w, ((1,), (1,)))

    enc = dot(hid, (part * slope).astype(BF16), ((0,), (0,))).astype(BF16)
    enc = enc.reshape(2, half, width)
    enc_mine = enc[core].astype(F32) + swap(enc[1 - core], "c").astype(F32)
    enc_mine = enc_mine.astype(BF16).reshape(16, half // 16, width)
    enc_mine = lax.all_to_all(enc_mine, ("y", "z"), 0, 0, tiled=True)
    enc_mine = jnp.sum(enc_mine.astype(F32), 0).astype(BF16)
    enc_x = lax.all_to_all(
        jnp.broadcast_to(enc_mine[None], (4,) + enc_mine.shape), ("xl", "xh"), 0, 0, tiled=True
    )
    enc_x = jnp.sum(enc_x.astype(F32), 0).astype(BF16)
    enc_half = lax.all_to_all(
        jnp.broadcast_to(enc_x[None], (16,) + enc_x.shape), ("y", "z"), 0, 0, tiled=True
    ).reshape(half, width)
    enc_rest = swap(enc_half, "c")
    enc_grad = jnp.where(
        core == 0, jnp.concatenate([enc_half, enc_rest]), jnp.concatenate([enc_rest, enc_half])
    ).astype(F32)

    sums = part.astype(BF16).reshape(n_peer, 2, rows, width)
    sums_mine = sums[:, core].astype(F32) + swap(sums[:, 1 - core], "c").astype(F32)
    got = lax.all_to_all(sums_mine.astype(BF16), ("y", "z", "xh"), 0, 0, tiled=True)
    emb_grad = jnp.sum(got.astype(F32), 0)
    act_own = jnp.tanh(dot(hidden, enc_weight, ((1,), (0,))))
    pre_grad = (emb_grad * (1.0 - act_own * act_own)).astype(BF16)
    input_grad = (emb_grad + dot(pre_grad, enc_weight, ((1,), (1,)))).astype(BF16)

    kept = [dot(emb_keep, e, ((0,), (0,))) for e in errs]
    cls_grad = jnp.concatenate(
        [(k + a.astype(F32)).astype(BF16) for k, a in zip(kept, arrived)], 1
    )
    return (cls_grad, input_grad, enc_grad)


def solution(mesh):
    grid = Mesh(mesh.devices.reshape(2, 4, 4, 2, 2), AXES)
    label = AXES[1:]
    placed = (P(AXES, None), P(), P(None, label), P("xl", label))
    return jax.shard_map(
        body,
        mesh=grid,
        in_specs=placed,
        out_specs=(P("xl", label), P(AXES, None), P()),
        check_vma=False,
    )
```

```python
import functools

import jax
import jax.numpy as jnp
from jax import lax
from jax.experimental import pallas as pl
from jax.experimental.pallas import tpu as pltpu
from jax.sharding import Mesh, PartitionSpec as P

F32 = jnp.float32
BF16 = jnp.bfloat16
AXES = ("xl", "y", "z", "xh", "c")
PLANE = ("y", "z")
CHUNKS = (768, 1024, 768, 512)
TILE = 256
MIB = 2**20
LIGHT = 1024
IN_VMEM = pl.BlockSpec(memory_space=pltpu.VMEM)
IN_SMEM = pl.BlockSpec(memory_space=pltpu.SMEM)
IN_HBM = pl.BlockSpec(memory_space=pl.ANY)


def dot(a, b, dims=((1,), (0,))):
    return lax.dot_general(a, b, (dims, ((), ())), preferred_element_type=F32)


def swap(x, axis):
    return lax.ppermute(x, axis, [(0, 1), (1, 0)])


def after(x, *earlier):
    return lax.optimization_barrier((x,) + earlier)[0]


def spread(x, axes, n):
    return lax.all_to_all(jnp.broadcast_to(x[None], (n,) + x.shape), axes, 0, 0, tiled=True)


def pick(x, i, dim=0):
    return lax.dynamic_index_in_dim(x, i, dim, keepdims=False)


def ring_pass(x, axis):
    me = lax.axis_index(axis)
    ring = [[(i, (i + k) % 4) for i in range(4)] for k in range(4)]
    return [pick(x, me)] + [lax.ppermute(pick(x, (me + k) % 4), axis, ring[k]) for k in (1, 2, 3)]


def add_up(blocks):
    return sum(b.astype(F32) for b in blocks)


def x_sum(x):
    there = [
        lax.ppermute(x, ("xl", "xh"), [(i, i ^ k) for i in range(4)]).astype(F32) for k in (1, 2, 3)
    ]
    return (x.astype(F32) + there[0]) + (there[1] + there[2])


def kernel_call(kernel, ins, places, outs, scratch=(), flops=0, moved=0, limit=20, **more):
    specs = {"s": IN_SMEM, "v": IN_VMEM, "h": IN_HBM}
    given = [
        pltpu.with_memory_space_constraint(x, pltpu.HBM) if p == "h" else x
        for x, p in zip(ins, places)
    ]
    return pl.pallas_call(
        kernel,
        out_shape=[o for _, o in outs],
        in_specs=[specs[p] for p in places],
        out_specs=[specs[p] for p, _ in outs],
        scratch_shapes=scratch,
        cost_estimate=pl.CostEstimate(flops=LIGHT, bytes_accessed=LIGHT, transcendentals=0),
        compiler_params=pltpu.CompilerParams(vmem_limit_bytes=limit * MIB),
        **more,
    )(*given)


def vmem(shape, dtype=BF16):
    return ("v", jax.ShapeDtypeStruct(shape, dtype))


def hbm(shape, dtype=BF16):
    return ("h", pltpu.HBM(shape, dtype))


def start_all(copies):
    for c in copies:
        c.start()
    return copies


def wait_all(copies):
    for c in copies:
        c.wait()


def cast_kernel(at, t_hbm, out, slots, done, in_sems, out_sems):
    n_slot, piece = slots.shape[0], slots.shape[1]
    per_core = t_hbm.shape[0] // piece
    steps = 2 * per_core

    def read(s):
        core = at[0] if s < per_core else 1 - at[0]
        src = t_hbm.at[pl.ds((s % per_core) * piece, piece), core]
        return pltpu.make_async_copy(src, slots.at[s % n_slot], in_sems.at[s % n_slot])

    def write(s):
        dst = out.at[pl.ds(s * piece, piece)]
        return pltpu.make_async_copy(done.at[s % n_slot], dst, out_sems.at[s % n_slot])

    for s in range(n_slot):
        read(s).start()
    for s in range(steps):
        read(s).wait()
        if s >= n_slot:
            write(s - n_slot).wait()
        done[s % n_slot] = slots[s % n_slot].astype(F32).astype(BF16)
        write(s).start()
        if s + n_slot < steps:
            read(s + n_slot).start()
    for s in range(steps - n_slot, steps):
        write(s).wait()


def cast_targets(at, targets, rows):
    labels = targets.shape[1]
    tall = targets.reshape(32, 2, rows, labels)
    (out,) = kernel_call(
        cast_kernel,
        (at, tall),
        "sh",
        [hbm((64, rows, labels))],
        scratch=[
            pltpu.VMEM((4, 4, rows, labels), jnp.int32),
            pltpu.VMEM((4, 4, rows, labels), BF16),
            pltpu.SemaphoreType.DMA((4,)),
            pltpu.SemaphoreType.DMA((4,)),
        ],
        flops=10**9,
        moved=6 * targets.size,
    )
    return out.reshape(64 * rows, labels)


def err_of(logits, t, scale):
    return ((jax.nn.sigmoid(logits) - t.astype(F32)) * scale).astype(BF16)


def front_kernel(
    scale, at, mine, other, enc_w, w_hbm, t_hbm,
    hid, emb, send_t, slope, err, w, t, keep_t, err_out, gone, keep_v, gone_v, sems,
):
    n, width = mine.shape
    half = width // 2
    first = err.shape[1]
    rest = w.shape[1] - first
    now, later = pl.ds(0, first), pl.ds(first, rest)
    halves = start_all([
        pltpu.make_async_copy(mine, hid.at[pl.ds(0, n)], sems.at[0]),
        pltpu.make_async_copy(other, hid.at[pl.ds(n, n)], sems.at[1]),
    ])
    chunk = start_all([
        pltpu.make_async_copy(w_hbm.at[:, now], w.at[:, now], sems.at[2]),
        pltpu.make_async_copy(t_hbm.at[:, now], t.at[:, now], sems.at[3]),
    ])
    others = start_all([
        pltpu.make_async_copy(w_hbm.at[:, later], w.at[:, later], sems.at[4]),
        pltpu.make_async_copy(t_hbm.at[:, later], t.at[:, later], sems.at[5]),
    ])
    for i, arrival in enumerate(halves):
        arrival.wait()
        rows = pl.ds(i * n, n)
        for d in range(0, width, TILE):
            cut = pl.ds(d, TILE)
            act = jnp.tanh(dot(hid[rows, :], enc_w[:, cut]))
            emb[rows, cut] = (hid[rows, cut].astype(F32) + act).astype(BF16)
            slope[rows, cut] = 1.0 - act * act
    first_half = emb[:, pl.ds(0, half)].T
    second_half = emb[:, pl.ds(half, half)].T
    low = at[1] == 0
    send_t[...] = jnp.where(low, second_half, first_half)
    keep_v[...] = jnp.where(low, first_half, second_half)
    leaving = start_all([pltpu.make_async_copy(keep_v, keep_t, sems.at[8])])
    wait_all(chunk)

    def tile(j, carry):
        cut = pl.ds(pl.multiple_of(j * TILE, TILE), TILE)
        e = err_of(dot(emb[...], w[:, cut]), t[:, cut], scale)
        err[:, cut] = e
        gone_v[:, cut] = dot(send_t[...], e).astype(BF16)
        return carry

    lax.fori_loop(0, first // TILE, tile, 0)
    leaving += start_all([
        pltpu.make_async_copy(gone_v, gone, sems.at[6]),
        pltpu.make_async_copy(err, err_out, sems.at[7]),
    ])
    wait_all(others + leaving)


def main_kernel(
    scale, at, hid, emb, send_t, slope, w, t, err0,
    enc_send, enc_keep, *refs,
):
    *gone, part_own, part_other, err_out, err, gone_v, parts_v, steep, sems = refs
    n_all, width = hid.shape
    half, n = width // 2, n_all // 2
    start = err0.shape[1]
    done = 0
    leaving = []
    for k, g in enumerate(gone):
        size = g.shape[1]

        def tile(j, carry):
            here = pl.multiple_of(done + j * TILE, TILE)
            cut, wide = pl.ds(here, TILE), pl.ds(here + start, TILE)
            e = err_of(dot(emb[...], w[:, wide]), t[:, wide], scale)
            err[:, cut] = e
            gone_v[:, cut] = dot(send_t[...], e).astype(BF16)
            return carry

        lax.fori_loop(0, size // TILE, tile, 0)
        leaving += start_all([pltpu.make_async_copy(gone_v.at[:, pl.ds(done, size)], g, sems.at[k])])
        done += size
    leaving += start_all([pltpu.make_async_copy(err, err_out, sems.at[len(gone) + 2])])
    transposed = ((1,), (1,))
    for i in (1, 0):
        rows = pl.ds(i * n, n)
        for d in range(0, width, TILE):
            cut = pl.ds(d, TILE)
            p = dot(err0[rows, :], w[cut, pl.ds(0, start)], transposed)
            p = p + dot(err[rows, :], w[cut, pl.ds(start, done)], transposed)
            parts_v[rows, cut] = p.astype(BF16)
            steep[rows, cut] = (p * slope[rows, cut]).astype(BF16)
        part = pltpu.make_async_copy(parts_v.at[rows], (part_own, part_other)[i], sems.at[len(gone) + i])
        leaving += start_all([part])
    low = at[0] == 0
    first, second = hid[:, pl.ds(0, half)].T, hid[:, pl.ds(half, half)].T
    for turned, out in (
        (jnp.where(low, second, first), enc_send),
        (jnp.where(low, first, second), enc_keep),
    ):
        for d in range(0, width, TILE):
            cut = pl.ds(d, TILE)
            out[:, cut] = dot(turned, steep[:, cut]).astype(out.dtype)
    wait_all(leaving)


def kept_kernel(pieces, again, keep_t, *refs):
    n = len(pieces)
    errs, come, refs = refs[:n], refs[n : 2 * n], refs[2 * n + again :]
    out, keep_v, err_v, come_v, out_v, sems = refs
    reads = [start_all([pltpu.make_async_copy(keep_t, keep_v, sems.at[0])])]
    cuts, at = [], 0
    for i, (lo, size, _) in enumerate(pieces):
        cut = pl.ds(at, size)
        reads.append(start_all([
            pltpu.make_async_copy(errs[i].at[:, pl.ds(lo, size)], err_v.at[:, cut], sems.at[3 * i + 1]),
            pltpu.make_async_copy(come[i], come_v.at[:, cut], sems.at[3 * i + 2]),
        ]))
        cuts.append(cut)
        at += size
    leaving = []
    wait_all(reads[0])
    at = 0
    for i, (_, size, start) in enumerate(pieces):
        wait_all(reads[i + 1])
        for d in range(at, at + size, TILE):
            cut = pl.ds(d, TILE)
            block = dot(keep_v[...], err_v[:, cut]) + come_v[:, cut].astype(F32)
            out_v[:, cut] = block.astype(BF16)
        at += size
        dst = out.at[:, pl.ds(start, size)]
        leaving += start_all([pltpu.make_async_copy(out_v.at[:, cuts[i]], dst, sems.at[3 * i + 3])])
    wait_all(leaving)


def keep_and_add(keep_t, pieces, labels, given=None):
    half, n_all = keep_t.shape
    size = sum(c.shape[1] for _, _, c, _ in pieces)
    n = len(pieces)
    again = given is not None
    ins = [keep_t] + [p[0] for p in pieces] + [p[2] for p in pieces] + ([given] if again else [])
    (out,) = kernel_call(
        functools.partial(kept_kernel, [(p[1], p[2].shape[1], p[3]) for p in pieces], int(again)),
        ins,
        "h" * len(ins),
        [hbm((half, labels))],
        scratch=[
            pltpu.VMEM((half, n_all), BF16),
            pltpu.VMEM((n_all, size), BF16),
            pltpu.VMEM((half, size), BF16),
            pltpu.VMEM((half, size), BF16),
            pltpu.SemaphoreType.DMA((3 * n + 1,)),
        ],
        input_output_aliases={len(ins) - 1: 0} if again else {},
    )
    return out


def body(hidden, enc_weight, cls_weight, targets):
    core = lax.axis_index("c")
    dp = lax.axis_index("xl")
    far = lax.axis_index("xh")
    at = jnp.stack([core, dp]).astype(jnp.int32)
    rows, width = hidden.shape
    labels = cls_weight.shape[1]
    half = width // 2
    n_all = 64 * rows
    n_own = n_all // 2
    scale = float(1.0 / (2048.0**0.5))

    mine = spread(hidden, ("y", "z", "xh"), 32)
    t = cast_targets(at, targets, rows)
    mine, t = lax.optimization_barrier((mine, t))
    other = swap(mine, "c").reshape(n_own, width)
    mine = mine.reshape(n_own, width)

    first, rest = CHUNKS[0], labels - CHUNKS[0]
    hid, emb, send_t, slope, err0, w_v, t_v, keep_t, err0_out, gone0 = kernel_call(
        functools.partial(front_kernel, scale),
        (at, mine, other, enc_weight, cls_weight, t),
        "shvvhh",
        [
            vmem((n_all, width)),
            vmem((n_all, width)),
            vmem((half, n_all)),
            vmem((n_all, width), F32),
            vmem((n_all, first)),
            vmem((width, labels)),
            vmem((n_all, labels)),
            hbm((half, n_all)),
            hbm((n_all, first)),
            hbm((half, first)),
        ],
        scratch=[
            pltpu.VMEM((half, n_all), BF16),
            pltpu.VMEM((half, first), BF16),
            pltpu.SemaphoreType.DMA((9,)),
        ],
        flops=2 * n_all * width * (width + first + first // 2),
        moved=4 * MIB,
    )
    gone0_in = swap(gone0, "xl")
    enc_send, enc_keep, *gone, part_own, part_other, err = kernel_call(
        functools.partial(main_kernel, scale),
        (at, hid, emb, send_t, slope, w_v, t_v, err0),
        "svvvvvvv",
        [vmem((half, width)), vmem((half, width), F32)]
        + [hbm((half, c)) for c in CHUNKS[1:]]
        + [hbm((n_own, width))] * 2
        + [hbm((n_all, rest))],
        scratch=[
            pltpu.VMEM((n_all, rest), BF16),
            pltpu.VMEM((half, rest), BF16),
            pltpu.VMEM((n_all, width), BF16),
            pltpu.VMEM((n_all, width), BF16),
            pltpu.SemaphoreType.DMA((len(CHUNKS) + 2,)),
        ],
        flops=2 * n_all * width * (rest + rest // 2 + labels + width),
        moved=8 * MIB,
    )
    enc_in = swap(after(enc_send, gone0_in), "c")
    gone1_in = swap(gone[0], "xl")

    enc = (enc_keep + enc_in.astype(F32)).astype(BF16)
    enc_sent = enc
    enc = lax.all_to_all(enc.reshape(16, half // 16, width), PLANE, 0, 0, tiled=True)
    cls_grad = keep_and_add(after(keep_t, enc_sent), [(err0_out, 0, gone0_in, 0)], labels)
    enc_part = jnp.sum(after(enc, gone1_in, cls_grad).astype(F32), 0).astype(BF16)
    enc = x_sum(enc_part).astype(BF16)
    gone2_in, gone3_in = swap(after(gone[1], enc), "xl"), swap(after(gone[2], enc), "xl")
    cls_grad = keep_and_add(after(keep_t, enc), [(err, 0, gone1_in, first)], labels, cls_grad)
    enc_half = after(spread(enc, PLANE, 16), gone2_in, cls_grad).reshape(half, width)
    enc_rest = swap(enc_half, "c")
    is_mine = (jnp.arange(2) == core)[:, None, None]
    enc_grad = jnp.where(is_mine, enc_half[None], enc_rest[None]).astype(F32).reshape(width, width)

    sums_in = swap(part_other, "c")
    sums = after((part_own.astype(F32) + sums_in.astype(F32)).astype(BF16), enc_sent)
    sums = [after(b, enc) for b in ring_pass(sums.reshape(4, 4 * 2 * rows, width), "y")]
    sums = add_up(sums).astype(BF16).reshape(4, 2 * rows, width)
    sums = [after(b, enc_half) for b in ring_pass(sums, "z")]
    sums = add_up(sums).reshape(2, rows, width)
    emb_grad = pick(sums, far) + swap(pick(sums, 1 - far).astype(BF16), "xh").astype(F32)
    act_own = jnp.tanh(dot(hidden, enc_weight))
    pre_grad = (emb_grad * (1.0 - act_own * act_own)).astype(BF16)
    input_grad = (emb_grad + dot(pre_grad, enc_weight, ((1,), (1,)))).astype(BF16)

    for come, start in ((gone2_in, sum(CHUNKS[:2])), (gone3_in, sum(CHUNKS[:3]))):
        cls_grad = keep_and_add(keep_t, [(err, start - first, come, start)], labels, cls_grad)
    return (cls_grad, input_grad, enc_grad)


def solution(mesh):
    grid = Mesh(mesh.devices.reshape(2, 4, 4, 2, 2), AXES)
    label = AXES[1:]
    placed = (P(AXES, None), P(), P(None, label), P("xl", label))
    return jax.shard_map(
        body,
        mesh=grid,
        in_specs=placed,
        out_specs=(P("xl", label), P(AXES, None), P()),
        check_vma=False,
    )
```

```python
import functools

import jax
import jax.numpy as jnp
from jax import lax
from jax.experimental import pallas as pl
from jax.experimental.pallas import tpu as pltpu
from jax.sharding import Mesh, PartitionSpec as P

F32 = jnp.float32
BF16 = jnp.bfloat16
AXES = ("xl", "y", "z", "xh", "c")
PLANE = ("y", "z")
CHUNKS = (768, 1024, 768, 512)
TILE = 256
MIB = 2**20
LIGHT = 1024
IN_VMEM = pl.BlockSpec(memory_space=pltpu.VMEM)
IN_SMEM = pl.BlockSpec(memory_space=pltpu.SMEM)
IN_HBM = pl.BlockSpec(memory_space=pl.ANY)


def dot(a, b, dims=((1,), (0,))):
    return lax.dot_general(a, b, (dims, ((), ())), preferred_element_type=F32)


def swap(x, axis):
    return lax.ppermute(x, axis, [(0, 1), (1, 0)])


def after(x, *earlier):
    return lax.optimization_barrier((x,) + earlier)[0]


def spread(x, axes, n):
    return lax.all_to_all(jnp.broadcast_to(x[None], (n,) + x.shape), axes, 0, 0, tiled=True)


def pick(x, i, dim=0):
    return lax.dynamic_index_in_dim(x, i, dim, keepdims=False)


def ring_pass(x, axis):
    me = lax.axis_index(axis)
    ring = [[(i, (i + k) % 4) for i in range(4)] for k in range(4)]
    return [pick(x, me)] + [lax.ppermute(pick(x, (me + k) % 4), axis, ring[k]) for k in (1, 2, 3)]


def add_up(blocks):
    return sum(b.astype(F32) for b in blocks)


def x_sum(x, *earlier):
    there = [lax.ppermute(x, ("xl", "xh"), [(i, i ^ k) for i in range(4)]) for k in (1, 2, 3)]
    there = [after(b, *earlier).astype(F32) for b in there]
    return (x.astype(F32) + there[0]) + (there[1] + there[2])


def kernel_call(kernel, ins, places, outs, scratch=(), flops=0, moved=0, limit=20, **more):
    specs = {"s": IN_SMEM, "v": IN_VMEM, "h": IN_HBM}
    given = [
        pltpu.with_memory_space_constraint(x, pltpu.HBM) if p == "h" else x
        for x, p in zip(ins, places)
    ]
    return pl.pallas_call(
        kernel,
        out_shape=[o for _, o in outs],
        in_specs=[specs[p] for p in places],
        out_specs=[specs[p] for p, _ in outs],
        scratch_shapes=scratch,
        cost_estimate=pl.CostEstimate(flops=LIGHT, bytes_accessed=LIGHT, transcendentals=0),
        compiler_params=pltpu.CompilerParams(vmem_limit_bytes=limit * MIB),
        **more,
    )(*given)


def vmem(shape, dtype=BF16):
    return ("v", jax.ShapeDtypeStruct(shape, dtype))


def hbm(shape, dtype=BF16):
    return ("h", pltpu.HBM(shape, dtype))


def start_all(copies):
    for c in copies:
        c.start()
    return copies


def wait_all(copies):
    for c in copies:
        c.wait()


def cast_kernel(at, t_hbm, out, slots, done, in_sems, out_sems):
    n_slot, piece = slots.shape[0], slots.shape[1]
    per_core = t_hbm.shape[0] // piece
    steps = 2 * per_core

    def read(s):
        core = at[0] if s < per_core else 1 - at[0]
        src = t_hbm.at[pl.ds((s % per_core) * piece, piece), core]
        return pltpu.make_async_copy(src, slots.at[s % n_slot], in_sems.at[s % n_slot])

    def write(s):
        dst = out.at[pl.ds(s * piece, piece)]
        return pltpu.make_async_copy(done.at[s % n_slot], dst, out_sems.at[s % n_slot])

    for s in range(n_slot):
        read(s).start()
    for s in range(steps):
        read(s).wait()
        if s >= n_slot:
            write(s - n_slot).wait()
        done[s % n_slot] = slots[s % n_slot].astype(F32).astype(BF16)
        write(s).start()
        if s + n_slot < steps:
            read(s + n_slot).start()
    for s in range(steps - n_slot, steps):
        write(s).wait()


def cast_targets(at, targets, rows):
    labels = targets.shape[1]
    tall = targets.reshape(32, 2, rows, labels)
    (out,) = kernel_call(
        cast_kernel,
        (at, tall),
        "sh",
        [hbm((64, rows, labels))],
        scratch=[
            pltpu.VMEM((4, 4, rows, labels), jnp.int32),
            pltpu.VMEM((4, 4, rows, labels), BF16),
            pltpu.SemaphoreType.DMA((4,)),
            pltpu.SemaphoreType.DMA((4,)),
        ],
        flops=10**9,
        moved=6 * targets.size,
    )
    return out.reshape(64 * rows, labels)


def err_of(logits, t, scale):
    return ((jax.nn.sigmoid(logits) - t.astype(F32)) * scale).astype(BF16)


def emb_rows(rows, hid, enc_w, emb, slope):
    for d in range(0, hid.shape[1], TILE):
        cut = pl.ds(d, TILE)
        act = jnp.tanh(dot(hid[...], enc_w[:, cut]))
        emb[rows, cut] = (hid[:, cut].astype(F32) + act).astype(BF16)
        slope[rows, cut] = (1.0 - act * act).astype(BF16)


def turn(rows, x, x_t):
    for d in range(0, x.shape[1], TILE):
        x_t[pl.ds(d, TILE), rows] = x[:, pl.ds(d, TILE)].T


def own_kernel(first, mine, enc_w, w_hbm, t_hbm, emb, slope, hid_t, emb_t, w, t, sems):
    n = mine.shape[0]
    now, rows = pl.ds(0, first), pl.ds(0, n)
    chunk = start_all([
        pltpu.make_async_copy(w_hbm.at[:, now], w.at[:, now], sems.at[0]),
        pltpu.make_async_copy(t_hbm.at[:, now], t.at[:, now], sems.at[1]),
    ])
    emb_rows(rows, mine, enc_w, emb, slope)
    turn(rows, mine, hid_t)
    turn(rows, emb.at[rows], emb_t)
    wait_all(chunk)


def both_halves(at, emb_t, err, lo, size, product):
    half = emb_t.shape[0] // 2
    for d in range(lo, lo + size, TILE):
        cut = pl.ds(d, TILE)
        product[:, cut] = dot(emb_t[...], err[:, cut]).astype(BF16)
    send = pl.ds(pl.multiple_of((1 - at[1]) * half, half), half)
    keep = pl.ds(pl.multiple_of(at[1] * half, half), half)
    return product.at[send, pl.ds(lo, size)], product.at[keep, pl.ds(lo, size)]


def front_kernel(
    scale, at, other, enc_w, w_hbm, t_hbm, emb0, slope0, hid_t0, emb_t0, w0, t0,
    emb, slope, hid_t, emb_t, w, t, err, gone, kept, product, sems,
):
    n = other.shape[0]
    first = err.shape[1]
    rows, later = pl.ds(n, n), pl.ds(first, w.shape[1] - first)
    copies = start_all([
        pltpu.make_async_copy(w_hbm.at[:, later], w.at[:, later], sems.at[0]),
        pltpu.make_async_copy(t_hbm.at[:, later], t.at[:, later], sems.at[1]),
    ])
    emb_rows(rows, other, enc_w, emb, slope)
    turn(rows, emb.at[rows], emb_t)
    for d in range(0, first, TILE):
        cut = pl.ds(d, TILE)
        err[:, cut] = err_of(dot(emb[...], w[:, cut]), t[:, cut], scale)
    send, keep = both_halves(at, emb_t, err, 0, first, product)
    copies += start_all([
        pltpu.make_async_copy(send, gone, sems.at[2]),
        pltpu.make_async_copy(keep, kept.at[:, pl.ds(0, first)], sems.at[3]),
    ])
    turn(rows, other, hid_t)
    wait_all(copies)


def main_kernel(scale, at, emb, slope, hid_t, emb_t, w, t, err0, kept0, *refs):
    enc_send, enc_keep, kept, part_own, part_other, *refs = refs
    *gone, err, product, parts_v, steep, sems = refs
    n_all, width = emb.shape
    half, n = width // 2, n_all // 2
    start, rest = err0.shape[1], err.shape[1]
    copies = []
    lo = 0
    for k, g in enumerate(gone):
        size = g.shape[1]
        for d in range(lo, lo + size, TILE):
            cut, wide = pl.ds(d, TILE), pl.ds(d + start, TILE)
            err[:, cut] = err_of(dot(emb[...], w[:, wide]), t[:, wide], scale)
        send, keep = both_halves(at, emb_t, err, lo, size, product)
        copies += start_all([
            pltpu.make_async_copy(send, g, sems.at[2 + 2 * k]),
            pltpu.make_async_copy(keep, kept.at[:, pl.ds(start + lo, size)], sems.at[3 + 2 * k]),
        ])
        lo += size
    transposed = ((1,), (1,))
    for i, part in ((1, part_other), (0, part_own)):
        rows = pl.ds(i * n, n)
        for d in range(0, width, TILE):
            cut = pl.ds(d, TILE)
            p = dot(err0[rows, :], w[cut, pl.ds(0, start)], transposed)
            p = p + dot(err[rows, :], w[cut, pl.ds(start, rest)], transposed)
            parts_v[rows, cut] = p.astype(BF16)
            steep[rows, cut] = (p * slope[rows, cut].astype(F32)).astype(BF16)
        copies += start_all([pltpu.make_async_copy(parts_v.at[rows], part, sems.at[i])])
    for lo, out in ((1 - at[0], enc_send), (at[0], enc_keep)):
        turned = pl.ds(pl.multiple_of(lo * half, half), half)
        for d in range(0, width, TILE):
            cut = pl.ds(d, TILE)
            out[:, cut] = dot(hid_t[turned, :], steep[:, cut]).astype(BF16)
    wait_all(copies)


def sum_kernel(a, b, out, total, sem):
    total[...] = (a[...].astype(F32) + b[...].astype(F32)).astype(BF16)
    copy = pltpu.make_async_copy(total, out, sem)
    copy.start()
    copy.wait()


def add_kernel(start, sizes, direct, kept, *refs):
    n = len(sizes)
    come, (out, mine, theirs, sems) = refs[:n], refs[n:]
    cuts = [pl.ds(sum(sizes[:i]), size) for i, size in enumerate(sizes)]
    places = [pl.ds(start + sum(sizes[:i]), size) for i, size in enumerate(sizes)]
    reads = []
    for i, (cut, place) in enumerate(zip(cuts, places)):
        reads.append(start_all([pltpu.make_async_copy(kept.at[:, place], mine.at[:, cut], sems.at[3 * i])]))
        if not direct:
            reads[i] += start_all([pltpu.make_async_copy(come[i], theirs.at[:, cut], sems.at[3 * i + 1])])
    writes = []
    for i, (cut, place) in enumerate(zip(cuts, places)):
        wait_all(reads[i])
        more = come[i][...] if direct else theirs[:, cut]
        mine[:, cut] = (mine[:, cut].astype(F32) + more.astype(F32)).astype(BF16)
        writes += start_all([pltpu.make_async_copy(mine.at[:, cut], out.at[:, place], sems.at[3 * i + 2])])
    wait_all(writes)


def add_in_place(kept, start, come, direct=False):
    half = kept.shape[0]
    sizes = [c.shape[1] for c in come]
    size = 0 if direct else sum(sizes)
    (out,) = kernel_call(
        functools.partial(add_kernel, start, sizes, direct),
        (kept, *come),
        "h" + ("v" if direct else "h") * len(come),
        [hbm(kept.shape)],
        scratch=[
            pltpu.VMEM((half, sum(sizes)), BF16),
            pltpu.VMEM((half, max(size, 128)), BF16),
            pltpu.SemaphoreType.DMA((3 * len(come),)),
        ],
        input_output_aliases={0: 0},
    )
    return out


def body(hidden, enc_weight, cls_weight, targets):
    core = lax.axis_index("c")
    dp = lax.axis_index("xl")
    far = lax.axis_index("xh")
    at = jnp.stack([core, dp]).astype(jnp.int32)
    rows, width = hidden.shape
    labels = cls_weight.shape[1]
    half = width // 2
    n_all = 64 * rows
    n_own = n_all // 2
    scale = float(1.0 / (2048.0**0.5))

    mine = spread(hidden, ("y", "z", "xh"), 32)
    t = cast_targets(at, targets, rows)
    mine, t = lax.optimization_barrier((mine, t))
    other = swap(mine, "c").reshape(n_own, width)
    mine = mine.reshape(n_own, width)

    first, rest = CHUNKS[0], labels - CHUNKS[0]
    starts = [sum(CHUNKS[:j]) for j in range(len(CHUNKS))]
    shared = [vmem((n_all, width))] * 2 + [vmem((width, n_all))] * 2
    shared += [vmem((width, labels)), vmem((n_all, labels))]
    half_done = kernel_call(
        functools.partial(own_kernel, first),
        (mine, enc_weight, cls_weight, t),
        "vvhh",
        shared,
        scratch=[pltpu.SemaphoreType.DMA((2,))],
    )
    *shared, err0, gone0, kept = kernel_call(
        functools.partial(front_kernel, scale),
        (at, other, enc_weight, cls_weight, t, *half_done),
        "svvhhvvvvvv",
        shared + [vmem((n_all, first)), hbm((half, first)), hbm((half, labels))],
        scratch=[pltpu.VMEM((width, first), BF16), pltpu.SemaphoreType.DMA((4,))],
        input_output_aliases={5 + i: i for i in range(6)},
    )
    gone0_in = swap(gone0, "xl")
    enc_send, enc_keep, kept, part_own, part_other, gone1, gone2, gone3 = kernel_call(
        functools.partial(main_kernel, scale),
        (at, *shared, err0, kept),
        "svvvvvvvh",
        [vmem((half, width))] * 2
        + [hbm((half, labels))]
        + [hbm((n_own, width))] * 2
        + [hbm((half, c)) for c in CHUNKS[1:]],
        scratch=[
            pltpu.VMEM((n_all, rest), BF16),
            pltpu.VMEM((width, rest), BF16),
            pltpu.VMEM((n_all, width), BF16),
            pltpu.VMEM((n_all, width), BF16),
            pltpu.SemaphoreType.DMA((2 * len(CHUNKS),)),
        ],
        input_output_aliases={8: 2},
    )
    enc_in = swap(after(enc_send, gone0_in), "c")
    gone1_in = swap(gone1, "xl")

    (enc_sent,) = kernel_call(
        sum_kernel,
        (enc_keep, enc_in),
        "vv",
        [hbm((half, width))],
        scratch=[pltpu.VMEM((half, width), BF16), pltpu.SemaphoreType.DMA],
    )
    enc = enc_sent
    enc = lax.all_to_all(enc.reshape(16, half // 16, width), PLANE, 0, 0, tiled=True)
    cls_grad = add_in_place(after(kept, enc_sent), 0, (gone0_in,))
    enc_part = jnp.sum(after(enc, gone1_in, cls_grad).astype(F32), 0).astype(BF16)

    sums_in = swap(part_other, "c")
    sums = after((part_own.astype(F32) + sums_in.astype(F32)).astype(BF16), enc_sent)
    sums = ring_pass(sums.reshape(4, 4 * 2 * rows, width), "y")

    enc = x_sum(enc_part, *sums[1:]).astype(BF16)
    gone2_in, gone3_in = swap(after(gone2, enc), "xl"), swap(after(gone3, enc), "xl")
    enc_half = after(spread(enc, PLANE, 16), gone2_in).reshape(half, width)
    enc_rest = swap(enc_half, "c")
    is_mine = (jnp.arange(2) == core)[:, None, None]
    enc_grad = jnp.where(is_mine, enc_half[None], enc_rest[None]).astype(F32).reshape(width, width)

    sums = [after(b, enc) for b in sums]
    sums = add_up(sums).astype(BF16).reshape(4, 2 * rows, width)
    sums = [after(b, enc_half) for b in ring_pass(sums, "z")]
    sums = add_up(sums).reshape(2, rows, width)
    emb_grad = pick(sums, far) + swap(pick(sums, 1 - far).astype(BF16), "xh").astype(F32)
    act_own = jnp.tanh(dot(hidden, enc_weight))
    pre_grad = (emb_grad * (1.0 - act_own * act_own)).astype(BF16)
    input_grad = (emb_grad + dot(pre_grad, enc_weight, ((1,), (1,)))).astype(BF16)

    cls_grad = add_in_place(after(cls_grad, enc_half), starts[1], (gone1_in, gone2_in))
    cls_grad = add_in_place(after(cls_grad, input_grad, enc_grad), starts[3], (gone3_in,), direct=True)
    return (cls_grad, input_grad, enc_grad)


def solution(mesh):
    grid = Mesh(mesh.devices.reshape(2, 4, 4, 2, 2), AXES)
    label = AXES[1:]
    placed = (P(AXES, None), P(), P(None, label), P("xl", label))
    return jax.shard_map(
        body,
        mesh=grid,
        in_specs=placed,
        out_specs=(P("xl", label), P(AXES, None), P()),
        check_vma=False,
    )
```

```python
import functools

import jax
import jax.numpy as jnp
from jax import lax
from jax.experimental import pallas as pl
from jax.experimental.pallas import tpu as pltpu
from jax.sharding import Mesh, PartitionSpec as P

F32 = jnp.float32
BF16 = jnp.bfloat16
AXES = ("xl", "y", "z", "xh", "c")
PLANE = ("y", "z")
CHUNKS = (768, 1024, 768, 512)
TILE = 256
MIB = 2**20
LIGHT = 1024
IN_VMEM = pl.BlockSpec(memory_space=pltpu.VMEM)
IN_SMEM = pl.BlockSpec(memory_space=pltpu.SMEM)
IN_HBM = pl.BlockSpec(memory_space=pl.ANY)


def dot(a, b, dims=((1,), (0,))):
    return lax.dot_general(a, b, (dims, ((), ())), preferred_element_type=F32)


def swap(x, axis):
    return lax.ppermute(x, axis, [(0, 1), (1, 0)])


def after(x, *earlier):
    return lax.optimization_barrier((x,) + earlier)[0]


def spread(x, axes, n):
    return lax.all_to_all(jnp.broadcast_to(x[None], (n,) + x.shape), axes, 0, 0, tiled=True)


def pick(x, i, dim=0):
    return lax.dynamic_index_in_dim(x, i, dim, keepdims=False)


def ring_pass(x, axis):
    me = lax.axis_index(axis)
    ring = [[(i, (i + k) % 4) for i in range(4)] for k in range(4)]
    return [pick(x, me)] + [lax.ppermute(pick(x, (me + k) % 4), axis, ring[k]) for k in (1, 2, 3)]


def add_up(blocks):
    return sum(b.astype(F32) for b in blocks)


def x_sum(x, *earlier):
    there = [lax.ppermute(x, ("xl", "xh"), [(i, i ^ k) for i in range(4)]) for k in (1, 2, 3)]
    there = [after(b, *earlier).astype(F32) for b in there]
    return (x.astype(F32) + there[0]) + (there[1] + there[2])


def kernel_call(kernel, ins, places, outs, scratch=(), flops=0, moved=0, limit=20, **more):
    specs = {"s": IN_SMEM, "v": IN_VMEM, "h": IN_HBM}
    given = [
        pltpu.with_memory_space_constraint(x, pltpu.HBM) if p == "h" else x
        for x, p in zip(ins, places)
    ]
    return pl.pallas_call(
        kernel,
        out_shape=[o for _, o in outs],
        in_specs=[specs[p] for p in places],
        out_specs=[specs[p] for p, _ in outs],
        scratch_shapes=scratch,
        cost_estimate=pl.CostEstimate(flops=LIGHT, bytes_accessed=LIGHT, transcendentals=0),
        compiler_params=pltpu.CompilerParams(vmem_limit_bytes=limit * MIB),
        **more,
    )(*given)


def vmem(shape, dtype=BF16):
    return ("v", jax.ShapeDtypeStruct(shape, dtype))


def hbm(shape, dtype=BF16):
    return ("h", pltpu.HBM(shape, dtype))


def start_all(copies):
    for c in copies:
        c.start()
    return copies


def wait_all(copies):
    for c in copies:
        c.wait()


def cast_kernel(at, t_hbm, out, slots, done, in_sems, out_sems):
    n_slot, piece = slots.shape[0], slots.shape[1]
    per_core = t_hbm.shape[0] // piece
    steps = 2 * per_core

    def read(s):
        core = at[0] if s < per_core else 1 - at[0]
        src = t_hbm.at[pl.ds((s % per_core) * piece, piece), core]
        return pltpu.make_async_copy(src, slots.at[s % n_slot], in_sems.at[s % n_slot])

    def write(s):
        dst = out.at[pl.ds(s * piece, piece)]
        return pltpu.make_async_copy(done.at[s % n_slot], dst, out_sems.at[s % n_slot])

    for s in range(n_slot):
        read(s).start()
    for s in range(steps):
        read(s).wait()
        if s >= n_slot:
            write(s - n_slot).wait()
        done[s % n_slot] = slots[s % n_slot].astype(F32).astype(BF16)
        write(s).start()
        if s + n_slot < steps:
            read(s + n_slot).start()
    for s in range(steps - n_slot, steps):
        write(s).wait()


def cast_targets(at, targets, rows):
    labels = targets.shape[1]
    tall = targets.reshape(32, 2, rows, labels)
    (out,) = kernel_call(
        cast_kernel,
        (at, tall),
        "sh",
        [hbm((64, rows, labels))],
        scratch=[
            pltpu.VMEM((4, 4, rows, labels), jnp.int32),
            pltpu.VMEM((4, 4, rows, labels), BF16),
            pltpu.SemaphoreType.DMA((4,)),
            pltpu.SemaphoreType.DMA((4,)),
        ],
        flops=10**9,
        moved=6 * targets.size,
    )
    return out.reshape(64 * rows, labels)


def err_of(logits, t, scale):
    sigmoid = pl.reciprocal(1.0 + jnp.exp(-logits))
    return ((sigmoid - t.astype(F32)) * scale).astype(BF16)


def emb_rows(rows, hid, enc_w, emb, slope):
    for d in range(0, hid.shape[1], TILE):
        cut = pl.ds(d, TILE)
        act = jnp.tanh(dot(hid[...], enc_w[:, cut]))
        emb[rows, cut] = (hid[:, cut].astype(F32) + act).astype(BF16)
        slope[rows, cut] = (1.0 - act * act).astype(BF16)


def turn(rows, x, x_t):
    for d in range(0, x.shape[1], TILE):
        x_t[pl.ds(d, TILE), rows] = x[:, pl.ds(d, TILE)].T


def own_kernel(first, mine, enc_w, w_hbm, t_hbm, emb, slope, hid_t, emb_t, w, t, sems):
    n = mine.shape[0]
    now, rows = pl.ds(0, first), pl.ds(0, n)
    chunk = start_all([
        pltpu.make_async_copy(w_hbm.at[:, now], w.at[:, now], sems.at[0]),
        pltpu.make_async_copy(t_hbm.at[:, now], t.at[:, now], sems.at[1]),
    ])
    emb_rows(rows, mine, enc_w, emb, slope)
    turn(rows, mine, hid_t)
    turn(rows, emb.at[rows], emb_t)
    wait_all(chunk)


def both_halves(at, emb_t, err, lo, size, product):
    half = emb_t.shape[0] // 2
    for d in range(lo, lo + size, TILE):
        cut = pl.ds(d, TILE)
        product[:, cut] = dot(emb_t[...], err[:, cut]).astype(BF16)
    send = pl.ds(pl.multiple_of((1 - at[1]) * half, half), half)
    keep = pl.ds(pl.multiple_of(at[1] * half, half), half)
    return product.at[send, pl.ds(lo, size)], product.at[keep, pl.ds(lo, size)]


def front_kernel(
    scale, at, other, enc_w, w_hbm, t_hbm, emb0, slope0, hid_t0, emb_t0, w0, t0,
    emb, slope, hid_t, emb_t, w, t, err, gone, kept, product, sems,
):
    n = other.shape[0]
    first = err.shape[1]
    rows, later = pl.ds(n, n), pl.ds(first, w.shape[1] - first)
    copies = start_all([
        pltpu.make_async_copy(w_hbm.at[:, later], w.at[:, later], sems.at[0]),
        pltpu.make_async_copy(t_hbm.at[:, later], t.at[:, later], sems.at[1]),
    ])
    emb_rows(rows, other, enc_w, emb, slope)
    turn(rows, emb.at[rows], emb_t)
    for d in range(0, first, TILE):
        cut = pl.ds(d, TILE)
        err[:, cut] = err_of(dot(emb[...], w[:, cut]), t[:, cut], scale)
    send, keep = both_halves(at, emb_t, err, 0, first, product)
    copies += start_all([
        pltpu.make_async_copy(send, gone, sems.at[2]),
        pltpu.make_async_copy(keep, kept.at[:, pl.ds(0, first)], sems.at[3]),
    ])
    turn(rows, other, hid_t)
    wait_all(copies)


def main_kernel(scale, at, emb, slope, hid_t, emb_t, w, t, err0, kept0, *refs):
    enc_send, enc_keep, kept, part_own, part_other, *refs = refs
    *gone, err, product, parts_v, steep, sems = refs
    n_all, width = emb.shape
    half, n = width // 2, n_all // 2
    start, rest = err0.shape[1], err.shape[1]
    copies = []
    lo = 0
    for k, g in enumerate(gone):
        size = g.shape[1]
        for d in range(lo, lo + size, TILE):
            cut, wide = pl.ds(d, TILE), pl.ds(d + start, TILE)
            err[:, cut] = err_of(dot(emb[...], w[:, wide]), t[:, wide], scale)
        send, keep = both_halves(at, emb_t, err, lo, size, product)
        copies += start_all([
            pltpu.make_async_copy(send, g, sems.at[2 + 2 * k]),
            pltpu.make_async_copy(keep, kept.at[:, pl.ds(start + lo, size)], sems.at[3 + 2 * k]),
        ])
        lo += size
    transposed = ((1,), (1,))
    for i, part in ((1, part_other), (0, part_own)):
        rows = pl.ds(i * n, n)
        for d in range(0, width, TILE):
            cut = pl.ds(d, TILE)
            p = dot(err0[rows, :], w[cut, pl.ds(0, start)], transposed)
            p = p + dot(err[rows, :], w[cut, pl.ds(start, rest)], transposed)
            parts_v[rows, cut] = p.astype(BF16)
            steep[rows, cut] = (p * slope[rows, cut].astype(F32)).astype(BF16)
        copies += start_all([pltpu.make_async_copy(parts_v.at[rows], part, sems.at[i])])
    for lo, out in ((1 - at[0], enc_send), (at[0], enc_keep)):
        turned = pl.ds(pl.multiple_of(lo * half, half), half)
        for d in range(0, width, TILE):
            cut = pl.ds(d, TILE)
            out[:, cut] = dot(hid_t[turned, :], steep[:, cut]).astype(BF16)
    wait_all(copies)


def sum_kernel(a, b, out, total, sem):
    total[...] = (a[...].astype(F32) + b[...].astype(F32)).astype(BF16)
    copy = pltpu.make_async_copy(total, out, sem)
    copy.start()
    copy.wait()


def add_kernel(start, sizes, direct, kept, *refs):
    n = len(sizes)
    come, (out, mine, theirs, sems) = refs[:n], refs[n:]
    cuts = [pl.ds(sum(sizes[:i]), size) for i, size in enumerate(sizes)]
    places = [pl.ds(start + sum(sizes[:i]), size) for i, size in enumerate(sizes)]
    reads = []
    for i, (cut, place) in enumerate(zip(cuts, places)):
        reads.append(start_all([pltpu.make_async_copy(kept.at[:, place], mine.at[:, cut], sems.at[3 * i])]))
        if not direct:
            reads[i] += start_all([pltpu.make_async_copy(come[i], theirs.at[:, cut], sems.at[3 * i + 1])])
    writes = []
    for i, (cut, place) in enumerate(zip(cuts, places)):
        wait_all(reads[i])
        more = come[i][...] if direct else theirs[:, cut]
        mine[:, cut] = (mine[:, cut].astype(F32) + more.astype(F32)).astype(BF16)
        writes += start_all([pltpu.make_async_copy(mine.at[:, cut], out.at[:, place], sems.at[3 * i + 2])])
    wait_all(writes)


def add_in_place(kept, start, come, direct=False):
    half = kept.shape[0]
    sizes = [c.shape[1] for c in come]
    size = 0 if direct else sum(sizes)
    (out,) = kernel_call(
        functools.partial(add_kernel, start, sizes, direct),
        (kept, *come),
        "h" + ("v" if direct else "h") * len(come),
        [hbm(kept.shape)],
        scratch=[
            pltpu.VMEM((half, sum(sizes)), BF16),
            pltpu.VMEM((half, max(size, 128)), BF16),
            pltpu.SemaphoreType.DMA((3 * len(come),)),
        ],
        input_output_aliases={0: 0},
    )
    return out


def body(hidden, enc_weight, cls_weight, targets):
    core = lax.axis_index("c")
    dp = lax.axis_index("xl")
    far = lax.axis_index("xh")
    at = jnp.stack([core, dp]).astype(jnp.int32)
    rows, width = hidden.shape
    labels = cls_weight.shape[1]
    half = width // 2
    n_all = 64 * rows
    n_own = n_all // 2
    scale = float(1.0 / (2048.0**0.5))

    mine = spread(hidden, ("y", "z", "xh"), 32)
    t = cast_targets(at, targets, rows)
    mine, t = lax.optimization_barrier((mine, t))
    other = swap(mine, "c").reshape(n_own, width)
    mine = mine.reshape(n_own, width)

    first, rest = CHUNKS[0], labels - CHUNKS[0]
    starts = [sum(CHUNKS[:j]) for j in range(len(CHUNKS))]
    shared = [vmem((n_all, width))] * 2 + [vmem((width, n_all))] * 2
    shared += [vmem((width, labels)), vmem((n_all, labels))]
    half_done = kernel_call(
        functools.partial(own_kernel, first),
        (mine, enc_weight, cls_weight, t),
        "vvhh",
        shared,
        scratch=[pltpu.SemaphoreType.DMA((2,))],
    )
    *shared, err0, gone0, kept = kernel_call(
        functools.partial(front_kernel, scale),
        (at, other, enc_weight, cls_weight, t, *half_done),
        "svvhhvvvvvv",
        shared + [vmem((n_all, first)), hbm((half, first)), hbm((half, labels))],
        scratch=[pltpu.VMEM((width, first), BF16), pltpu.SemaphoreType.DMA((4,))],
        input_output_aliases={5 + i: i for i in range(6)},
    )
    gone0_in = swap(gone0, "xl")
    enc_send, enc_keep, kept, part_own, part_other, gone1, gone2, gone3 = kernel_call(
        functools.partial(main_kernel, scale),
        (at, *shared, err0, kept),
        "svvvvvvvh",
        [vmem((half, width))] * 2
        + [hbm((half, labels))]
        + [hbm((n_own, width))] * 2
        + [hbm((half, c)) for c in CHUNKS[1:]],
        scratch=[
            pltpu.VMEM((n_all, rest), BF16),
            pltpu.VMEM((width, rest), BF16),
            pltpu.VMEM((n_all, width), BF16),
            pltpu.VMEM((n_all, width), BF16),
            pltpu.SemaphoreType.DMA((2 * len(CHUNKS),)),
        ],
        input_output_aliases={8: 2},
    )
    enc_in = swap(after(enc_send, gone0_in), "c")
    gone1_in = swap(gone1, "xl")

    (enc_sent,) = kernel_call(
        sum_kernel,
        (enc_keep, enc_in),
        "vv",
        [hbm((half, width))],
        scratch=[pltpu.VMEM((half, width), BF16), pltpu.SemaphoreType.DMA],
    )
    enc = enc_sent
    enc = lax.all_to_all(enc.reshape(16, half // 16, width), PLANE, 0, 0, tiled=True)
    cls_grad = add_in_place(after(kept, enc_sent), 0, (gone0_in,))
    enc_part = jnp.sum(after(enc, gone1_in, cls_grad).astype(F32), 0).astype(BF16)

    sums_in = swap(part_other, "c")
    sums = after((part_own.astype(F32) + sums_in.astype(F32)).astype(BF16), enc_sent)
    sums = ring_pass(sums.reshape(4, 4 * 2 * rows, width), "y")

    enc = x_sum(enc_part, *sums[1:]).astype(BF16)
    gone2_in, gone3_in = swap(after(gone2, enc), "xl"), swap(after(gone3, enc), "xl")
    enc_half = after(spread(enc, PLANE, 16), gone2_in).reshape(half, width)
    enc_rest = swap(enc_half, "c")
    is_mine = (jnp.arange(2) == core)[:, None, None]
    enc_grad = jnp.where(is_mine, enc_half[None], enc_rest[None]).astype(F32).reshape(width, width)

    sums = [after(b, enc) for b in sums]
    sums = add_up(sums).astype(BF16).reshape(4, 2 * rows, width)
    sums = [after(b, enc_half) for b in ring_pass(sums, "z")]
    sums = add_up(sums).reshape(2, rows, width)
    emb_grad = pick(sums, far) + swap(pick(sums, 1 - far).astype(BF16), "xh").astype(F32)
    act_own = jnp.tanh(dot(hidden, enc_weight))
    pre_grad = (emb_grad * (1.0 - act_own * act_own)).astype(BF16)
    input_grad = (emb_grad + dot(pre_grad, enc_weight, ((1,), (1,)))).astype(BF16)

    cls_grad = add_in_place(after(cls_grad, enc_half), starts[1], (gone1_in, gone2_in))
    cls_grad = add_in_place(after(cls_grad, input_grad, enc_grad), starts[3], (gone3_in,), direct=True)
    return (cls_grad, input_grad, enc_grad)


def solution(mesh):
    grid = Mesh(mesh.devices.reshape(2, 4, 4, 2, 2), AXES)
    label = AXES[1:]
    placed = (P(AXES, None), P(), P(None, label), P("xl", label))
    return jax.shard_map(
        body,
        mesh=grid,
        in_specs=placed,
        out_specs=(P("xl", label), P(AXES, None), P()),
        check_vma=False,
    )
```

```python
import functools

import jax
import jax.numpy as jnp
from jax import lax
from jax.experimental import pallas as pl
from jax.experimental.pallas import tpu as pltpu
from jax.sharding import Mesh, PartitionSpec as P

F32 = jnp.float32
BF16 = jnp.bfloat16
AXES = ("xl", "y", "z", "xh", "c")
PLANE = ("y", "z")
CHUNKS = (768, 1024, 768, 512)
TILE = 256
MIB = 2**20
LIGHT = 1024
IN_VMEM = pl.BlockSpec(memory_space=pltpu.VMEM)
IN_SMEM = pl.BlockSpec(memory_space=pltpu.SMEM)
IN_HBM = pl.BlockSpec(memory_space=pl.ANY)


def dot(a, b, dims=((1,), (0,))):
    return lax.dot_general(a, b, (dims, ((), ())), preferred_element_type=F32)


def swap(x, axis):
    return lax.ppermute(x, axis, [(0, 1), (1, 0)])


def after(x, *earlier):
    return lax.optimization_barrier((x,) + earlier)[0]


def spread(x, axes, n):
    return lax.all_to_all(jnp.broadcast_to(x[None], (n,) + x.shape), axes, 0, 0, tiled=True)


def pick(x, i, dim=0):
    return lax.dynamic_index_in_dim(x, i, dim, keepdims=False)


def ring_pass(x, axis):
    me = lax.axis_index(axis)
    ring = [[(i, (i + k) % 4) for i in range(4)] for k in range(4)]
    return [pick(x, me)] + [lax.ppermute(pick(x, (me + k) % 4), axis, ring[k]) for k in (1, 2, 3)]


def add_up(blocks):
    return sum(b.astype(F32) for b in blocks)


def x_sum(x, *earlier):
    there = [lax.ppermute(x, ("xl", "xh"), [(i, i ^ k) for i in range(4)]) for k in (1, 2, 3)]
    there = [after(b, *earlier).astype(F32) for b in there]
    return (x.astype(F32) + there[0]) + (there[1] + there[2])


def kernel_call(kernel, ins, places, outs, scratch=(), flops=0, moved=0, limit=20, **more):
    specs = {"s": IN_SMEM, "v": IN_VMEM, "h": IN_HBM}
    given = [
        pltpu.with_memory_space_constraint(x, pltpu.HBM) if p == "h" else x
        for x, p in zip(ins, places)
    ]
    return pl.pallas_call(
        kernel,
        out_shape=[o for _, o in outs],
        in_specs=[specs[p] for p in places],
        out_specs=[specs[p] for p, _ in outs],
        scratch_shapes=scratch,
        cost_estimate=pl.CostEstimate(flops=LIGHT, bytes_accessed=LIGHT, transcendentals=0),
        compiler_params=pltpu.CompilerParams(vmem_limit_bytes=limit * MIB),
        **more,
    )(*given)


def vmem(shape, dtype=BF16):
    return ("v", jax.ShapeDtypeStruct(shape, dtype))


def hbm(shape, dtype=BF16):
    return ("h", pltpu.HBM(shape, dtype))


def start_all(copies):
    for c in copies:
        c.start()
    return copies


def wait_all(copies):
    for c in copies:
        c.wait()


def cast_kernel(at, t_hbm, out, slots, done, in_sems, out_sems):
    n_slot, piece = slots.shape[0], slots.shape[1]
    per_core = t_hbm.shape[0] // piece
    steps = 2 * per_core

    def read(s):
        core = at[0] if s < per_core else 1 - at[0]
        src = t_hbm.at[pl.ds((s % per_core) * piece, piece), core]
        return pltpu.make_async_copy(src, slots.at[s % n_slot], in_sems.at[s % n_slot])

    def write(s):
        dst = out.at[pl.ds(s * piece, piece)]
        return pltpu.make_async_copy(done.at[s % n_slot], dst, out_sems.at[s % n_slot])

    for s in range(n_slot):
        read(s).start()
    for s in range(steps):
        read(s).wait()
        if s >= n_slot:
            write(s - n_slot).wait()
        done[s % n_slot] = slots[s % n_slot].astype(F32).astype(BF16)
        write(s).start()
        if s + n_slot < steps:
            read(s + n_slot).start()
    for s in range(steps - n_slot, steps):
        write(s).wait()


def cast_targets(at, targets, rows):
    labels = targets.shape[1]
    tall = targets.reshape(32, 2, rows, labels)
    (out,) = kernel_call(
        cast_kernel,
        (at, tall),
        "sh",
        [hbm((64, rows, labels))],
        scratch=[
            pltpu.VMEM((4, 4, rows, labels), jnp.int32),
            pltpu.VMEM((4, 4, rows, labels), BF16),
            pltpu.SemaphoreType.DMA((4,)),
            pltpu.SemaphoreType.DMA((4,)),
        ],
        flops=10**9,
        moved=6 * targets.size,
    )
    return out.reshape(64 * rows, labels)


def err_of(logits, t, scale):
    sigmoid = pl.reciprocal(1.0 + jnp.exp(-logits))
    return ((sigmoid - t.astype(F32)) * scale).astype(BF16)


def emb_rows(rows, hid, enc_w, emb, slope):
    for d in range(0, hid.shape[1], TILE):
        cut = pl.ds(d, TILE)
        act = jnp.tanh(dot(hid[...], enc_w[:, cut]))
        emb[rows, cut] = (hid[:, cut].astype(F32) + act).astype(BF16)
        slope[rows, cut] = (1.0 - act * act).astype(BF16)


def turn(rows, x, x_t):
    for d in range(0, x.shape[1], TILE):
        x_t[pl.ds(d, TILE), rows] = x[:, pl.ds(d, TILE)].T


def own_kernel(first, mine, enc_w, w_hbm, t_hbm, emb, slope, hid_t, emb_t, w, t, sems):
    n = mine.shape[0]
    now, rows = pl.ds(0, first), pl.ds(0, n)
    chunk = start_all([
        pltpu.make_async_copy(w_hbm.at[:, now], w.at[:, now], sems.at[0]),
        pltpu.make_async_copy(t_hbm.at[:, now], t.at[:, now], sems.at[1]),
    ])
    emb_rows(rows, mine, enc_w, emb, slope)
    turn(rows, mine, hid_t)
    turn(rows, emb.at[rows], emb_t)
    wait_all(chunk)


def both_halves(at, emb_t, err, lo, size, product):
    half = emb_t.shape[0] // 2
    for d in range(lo, lo + size, TILE):
        cut = pl.ds(d, TILE)
        product[:, cut] = dot(emb_t[...], err[:, cut]).astype(BF16)
    send = pl.ds(pl.multiple_of((1 - at[1]) * half, half), half)
    keep = pl.ds(pl.multiple_of(at[1] * half, half), half)
    return product.at[send, pl.ds(lo, size)], product.at[keep, pl.ds(lo, size)]


def front_kernel(
    scale, at, other, enc_w, w_hbm, t_hbm, emb0, slope0, hid_t0, emb_t0, w0, t0,
    emb, slope, hid_t, emb_t, w, t, err, gone, kept, product, sems,
):
    n = other.shape[0]
    first = err.shape[1]
    rows, later = pl.ds(n, n), pl.ds(first, w.shape[1] - first)
    copies = start_all([
        pltpu.make_async_copy(w_hbm.at[:, later], w.at[:, later], sems.at[0]),
        pltpu.make_async_copy(t_hbm.at[:, later], t.at[:, later], sems.at[1]),
    ])
    emb_rows(rows, other, enc_w, emb, slope)
    turn(rows, emb.at[rows], emb_t)
    for d in range(0, first, TILE):
        cut = pl.ds(d, TILE)
        err[:, cut] = err_of(dot(emb[...], w[:, cut]), t[:, cut], scale)
    send, keep = both_halves(at, emb_t, err, 0, first, product)
    copies += start_all([
        pltpu.make_async_copy(send, gone, sems.at[2]),
        pltpu.make_async_copy(keep, kept.at[:, pl.ds(0, first)], sems.at[3]),
    ])
    turn(rows, other, hid_t)
    wait_all(copies)


def main_kernel(scale, at, emb, slope, hid_t, emb_t, w, t, err0, kept0, *refs):
    enc_send, enc_keep, kept, part_own, part_other, *refs = refs
    *gone, err, product, parts_v, steep, sems = refs
    n_all, width = emb.shape
    half, n = width // 2, n_all // 2
    start, rest = err0.shape[1], err.shape[1]
    copies = []
    lo = 0
    for k, g in enumerate(gone):
        size = g.shape[1]
        for d in range(lo, lo + size, TILE):
            cut, wide = pl.ds(d, TILE), pl.ds(d + start, TILE)
            err[:, cut] = err_of(dot(emb[...], w[:, wide]), t[:, wide], scale)
        send, keep = both_halves(at, emb_t, err, lo, size, product)
        copies += start_all([
            pltpu.make_async_copy(send, g, sems.at[2 + 2 * k]),
            pltpu.make_async_copy(keep, kept.at[:, pl.ds(start + lo, size)], sems.at[3 + 2 * k]),
        ])
        lo += size
    transposed = ((1,), (1,))
    for i, part in ((1, part_other), (0, part_own)):
        rows = pl.ds(i * n, n)
        for d in range(0, width, TILE):
            cut = pl.ds(d, TILE)
            p = dot(err0[rows, :], w[cut, pl.ds(0, start)], transposed)
            p = p + dot(err[rows, :], w[cut, pl.ds(start, rest)], transposed)
            parts_v[rows, cut] = p.astype(BF16)
            steep[rows, cut] = (p * slope[rows, cut].astype(F32)).astype(BF16)
        copies += start_all([pltpu.make_async_copy(parts_v.at[rows], part, sems.at[i])])
    for lo, out in ((1 - at[0], enc_send), (at[0], enc_keep)):
        turned = pl.ds(pl.multiple_of(lo * half, half), half)
        for d in range(0, width, TILE):
            cut = pl.ds(d, TILE)
            out[:, cut] = dot(hid_t[turned, :], steep[:, cut]).astype(BF16)
    wait_all(copies)


def sum_kernel(a, b, out, total, sem):
    total[...] = (a[...].astype(F32) + b[...].astype(F32)).astype(BF16)
    copy = pltpu.make_async_copy(total, out, sem)
    copy.start()
    copy.wait()


def add_parts(sizes, direct):
    step = TILE if direct else 2 * TILE
    return [
        (i, pl.ds(d, min(step, size - d)), pl.ds(sum(sizes[:i]) + d, min(step, size - d)))
        for i, size in enumerate(sizes)
        for d in range(0, size, step)
    ]


def add_kernel(start, sizes, direct, kept, *refs):
    n = len(sizes)
    come, (out, mine, theirs, sems) = refs[:n], refs[n:]
    parts = add_parts(sizes, direct)
    places = [pl.ds(start + cut.start, cut.size) for _, _, cut in parts]
    reads = []
    for k, (i, its, cut) in enumerate(parts):
        reads.append(start_all([pltpu.make_async_copy(kept.at[:, places[k]], mine.at[:, cut], sems.at[3 * k])]))
        if not direct:
            there = pltpu.make_async_copy(come[i].at[:, its], theirs.at[:, cut], sems.at[3 * k + 1])
            reads[k] += start_all([there])
    writes = []
    for k, (i, its, cut) in enumerate(parts):
        wait_all(reads[k])
        more = come[i][:, its] if direct else theirs[:, cut]
        mine[:, cut] = (mine[:, cut].astype(F32) + more.astype(F32)).astype(BF16)
        writes += start_all([pltpu.make_async_copy(mine.at[:, cut], out.at[:, places[k]], sems.at[3 * k + 2])])
    wait_all(writes)


def add_in_place(kept, start, come, direct=False):
    half = kept.shape[0]
    sizes = [c.shape[1] for c in come]
    size = 0 if direct else sum(sizes)
    (out,) = kernel_call(
        functools.partial(add_kernel, start, sizes, direct),
        (kept, *come),
        "h" + ("v" if direct else "h") * len(come),
        [hbm(kept.shape)],
        scratch=[
            pltpu.VMEM((half, sum(sizes)), BF16),
            pltpu.VMEM((half, max(size, 128)), BF16),
            pltpu.SemaphoreType.DMA((3 * len(add_parts(sizes, direct)),)),
        ],
        input_output_aliases={0: 0},
    )
    return out


def body(hidden, enc_weight, cls_weight, targets):
    core = lax.axis_index("c")
    dp = lax.axis_index("xl")
    far = lax.axis_index("xh")
    at = jnp.stack([core, dp]).astype(jnp.int32)
    rows, width = hidden.shape
    labels = cls_weight.shape[1]
    half = width // 2
    n_all = 64 * rows
    n_own = n_all // 2
    scale = float(1.0 / (2048.0**0.5))

    mine = spread(hidden, ("y", "z", "xh"), 32)
    t = cast_targets(at, targets, rows)
    mine, t = lax.optimization_barrier((mine, t))
    other = swap(mine, "c").reshape(n_own, width)
    mine = mine.reshape(n_own, width)

    first, rest = CHUNKS[0], labels - CHUNKS[0]
    starts = [sum(CHUNKS[:j]) for j in range(len(CHUNKS))]
    shared = [vmem((n_all, width))] * 2 + [vmem((width, n_all))] * 2
    shared += [vmem((width, labels)), vmem((n_all, labels))]
    half_done = kernel_call(
        functools.partial(own_kernel, first),
        (mine, enc_weight, cls_weight, t),
        "vvhh",
        shared,
        scratch=[pltpu.SemaphoreType.DMA((2,))],
    )
    *shared, err0, gone0, kept = kernel_call(
        functools.partial(front_kernel, scale),
        (at, other, enc_weight, cls_weight, t, *half_done),
        "svvhhvvvvvv",
        shared + [vmem((n_all, first)), hbm((half, first)), hbm((half, labels))],
        scratch=[pltpu.VMEM((width, first), BF16), pltpu.SemaphoreType.DMA((4,))],
        input_output_aliases={5 + i: i for i in range(6)},
    )
    gone0_in = swap(gone0, "xl")
    enc_send, enc_keep, kept, part_own, part_other, gone1, gone2, gone3 = kernel_call(
        functools.partial(main_kernel, scale),
        (at, *shared, err0, kept),
        "svvvvvvvh",
        [vmem((half, width))] * 2
        + [hbm((half, labels))]
        + [hbm((n_own, width))] * 2
        + [hbm((half, c)) for c in CHUNKS[1:]],
        scratch=[
            pltpu.VMEM((n_all, rest), BF16),
            pltpu.VMEM((width, rest), BF16),
            pltpu.VMEM((n_all, width), BF16),
            pltpu.VMEM((n_all, width), BF16),
            pltpu.SemaphoreType.DMA((2 * len(CHUNKS),)),
        ],
        input_output_aliases={8: 2},
    )
    enc_in = swap(after(enc_send, gone0_in), "c")
    gone1_in = swap(gone1, "xl")

    (enc_sent,) = kernel_call(
        sum_kernel,
        (enc_keep, enc_in),
        "vv",
        [hbm((half, width))],
        scratch=[pltpu.VMEM((half, width), BF16), pltpu.SemaphoreType.DMA],
    )
    enc = enc_sent
    enc = lax.all_to_all(enc.reshape(16, half // 16, width), PLANE, 0, 0, tiled=True)
    cls_grad = add_in_place(after(kept, enc_sent), 0, (gone0_in,))
    enc_part = jnp.sum(after(enc, gone1_in, cls_grad).astype(F32), 0).astype(BF16)

    sums_in = swap(part_other, "c")
    sums = after((part_own.astype(F32) + sums_in.astype(F32)).astype(BF16), enc_sent)
    sums = ring_pass(sums.reshape(4, 4 * 2 * rows, width), "y")

    enc = x_sum(enc_part, *sums[1:]).astype(BF16)
    gone2_in, gone3_in = swap(after(gone2, enc), "xl"), swap(after(gone3, enc), "xl")
    enc_half = after(spread(enc, PLANE, 16), gone2_in).reshape(half, width)
    enc_rest = swap(enc_half, "c")
    is_mine = (jnp.arange(2) == core)[:, None, None]
    enc_grad = jnp.where(is_mine, enc_half[None], enc_rest[None]).astype(F32).reshape(width, width)

    sums = [after(b, enc) for b in sums]
    sums = add_up(sums).astype(BF16).reshape(4, 2 * rows, width)
    sums = [after(b, enc_half) for b in ring_pass(sums, "z")]
    sums = add_up(sums).reshape(2, rows, width)
    emb_grad = pick(sums, far) + swap(pick(sums, 1 - far).astype(BF16), "xh").astype(F32)
    act_own = jnp.tanh(dot(hidden, enc_weight))
    pre_grad = (emb_grad * (1.0 - act_own * act_own)).astype(BF16)
    input_grad = (emb_grad + dot(pre_grad, enc_weight, ((1,), (1,)))).astype(BF16)

    cls_grad = add_in_place(after(cls_grad, enc_half), starts[1], (gone1_in, gone2_in))
    cls_grad = add_in_place(after(cls_grad, input_grad, enc_grad), starts[3], (gone3_in,), direct=True)
    return (cls_grad, input_grad, enc_grad)


def solution(mesh):
    grid = Mesh(mesh.devices.reshape(2, 4, 4, 2, 2), AXES)
    label = AXES[1:]
    placed = (P(AXES, None), P(), P(None, label), P("xl", label))
    return jax.shard_map(
        body,
        mesh=grid,
        in_specs=placed,
        out_specs=(P("xl", label), P(AXES, None), P()),
        check_vma=False,
    )
```
